256 devices in a mesh: ka: 64 (over x, z, y_hi), ea: 4 (over y_lo, core).
Axes of the slice: x: 4, y: 4 (y_hi: 2, y_lo: 2; y = y_hi * 2 + y_lo), z: 8, core: 2. Of those that a mesh axis runs over, the one named last changes fastest.
Arguments:
- lesser: bfloat16 [64, 8, 192, 384], P('ka', 'ea'), may hold values from -6 to 6
- greater: bfloat16 [64, 8, 192, 384], P('ka', 'ea'), may hold values from -6 to 6
- coupling: bfloat16 [192, 384], replicated, may hold values from -0.3125 to 0.3125
- cotangent: bfloat16 [9, 4, 192, 384], replicated, may hold values from -0.0546875 to 0.0546875
- offsets: int32 [9], replicated, may hold values from 0 to 8, each once
- mode_shift: int32 [4], replicated, may hold values from 1 to 2, as said below
Outputs:
- grad_lesser: bfloat16 [64, 8, 192, 384], P('ka', 'ea')
- grad_greater: bfloat16 [64, 8, 192, 384], P('ka', 'ea')
The draws below stay inside these ranges and needn't reach their ends.
Inputs may be any that keep to these rules, and one draw needn't show every extreme that they name: `offsets`: each value 0 to 8 stands once. `mode_shift`: at least one mode has the shift 2.
All inputs are finite; a program needn't handle non-finite values.
Results may differ from the reference program's by a relative error of at most 0.0058.
Values may be sent and summed in bfloat16 or wider, within the bound.
No kernel may reach another device: no remote copies, remote signals or barrier semaphores. Data moves between devices by JAX's collectives and lax.ppermute only.
A program may use at most 128 MiB of HBM per device.

```python
import jax
import jax.numpy as jnp
from jax import lax

NO = 192
QS = 4
NM = 4
SMAX = 2
QN = 9
KPTS = 64
ENERGIES = 8


def draw_mode_shift(key, part):
    first_key, second_key = jax.random.split(jax.random.fold_in(key, 17))
    values = jax.random.randint(first_key, (NM,), 1, SMAX + 1)
    chosen = jax.random.randint(second_key, (), 0, NM)
    return jnp.where(jnp.arange(NM) == chosen, SMAX, values).astype(jnp.int32)


def block_levels(own_key, extent, cuts, low, top_value):
    level = 1.0
    for dim, parts in cuts:
        draws = jax.random.uniform(jax.random.fold_in(jax.random.fold_in(own_key, 6), dim), (parts,), jnp.float32, low / len(cuts), top_value / len(cuts))
        level = level * jnp.repeat(jnp.exp(draws), extent[dim] // parts).reshape((-1,) + (1,) * (len(extent) - 1 - dim))
    return level


def normal_values(rng, extent, scale, bound, cuts=(), kind=jnp.bfloat16):
    entries = jax.random.normal(rng, extent, jnp.float32) * scale
    if len(cuts) > 0:
        entries = block_levels(rng, extent, cuts, -0.22, 0.18) * entries
    return jnp.clip(entries, min=-bound, max=bound).astype(kind)


def setup_inputs(seed: int = 0) -> dict:
    splits = jax.random.split(jax.random.key(seed), 7)
    return {
        "lesser": normal_values(splits[0], (KPTS, ENERGIES, NO, 2 * NO), 1.0, 6.0, ((0, 64), (1, 4))),
        "greater": normal_values(splits[1], (KPTS, ENERGIES, NO, 2 * NO), 1.0, 6.0, ((0, 64), (1, 4))),
        "coupling": normal_values(splits[2], (NO, 2 * NO), (2 * NO) ** -0.5, 0.3125),
        "cotangent": normal_values(splits[3], (QN, NM, NO, 2 * NO), (2 * NO * QN * NM) ** -0.5, 0.0546875),
        "offsets": jax.random.permutation(splits[4], QN).astype(jnp.int32),
        "mode_shift": draw_mode_shift(jax.random.fold_in(splits[6], 71), 0),
    }


def bigform(block):
    width = block.shape[-1] // 2
    real_part = block[..., :width]
    imag_part = block[..., width:]
    upper_half = jnp.concatenate([real_part, imag_part], -1)
    lower_half = jnp.concatenate([-imag_part, real_part], -1)
    return jnp.concatenate([upper_half, lower_half], -2)


def conjugate(block):
    width = block.shape[-1] // 2
    real_part = jnp.swapaxes(block[..., :width], -1, -2)
    imag_part = jnp.swapaxes(block[..., width:], -1, -2)
    return jnp.concatenate([real_part, -imag_part], -1)


def product(left, right_big):
    block_shape = left.shape
    flattened = left.reshape(-1, block_shape[-1])
    result = jnp.dot(flattened, right_big, preferred_element_type=jnp.float32)
    return result.reshape(block_shape[:-1] + (right_big.shape[-1],))


def sandwich(blocks, big_c, big_ch):
    half_block = product(blocks, big_c).astype(jnp.bfloat16)
    return product(conjugate(half_block), big_ch).astype(jnp.bfloat16)


def reference(lesser, greater, coupling, cotangent, offsets, mode_shift):
    big_c = bigform(coupling)
    big_ch = bigform(conjugate(coupling))
    flipped = sandwich(lesser, big_c, big_ch)
    big_p = bigform(cotangent)
    big_ph = jnp.swapaxes(big_p, -1, -2)
    slot_of = jnp.argsort(offsets).astype(jnp.int32)
    padded_up = jnp.pad(flipped, ((0, 0), (0, SMAX), (0, 0), (0, 0)))
    padded_down = jnp.pad(greater, ((0, 0), (SMAX, 0), (0, 0), (0, 0)))
    total_lesser = jnp.zeros(lesser.shape, jnp.float32)
    total_greater = jnp.zeros(lesser.shape, jnp.float32)
    for offset in range(-QS, QS + 1):
        slot_index = slot_of[offset + QS]
        upper_blocks = jnp.roll(padded_up, -offset, axis=0)
        lower_blocks = jnp.roll(padded_down, offset, axis=0)
        for phonon in range(NM):
            shift = mode_shift[phonon].astype(jnp.int32)
            upper_part = lax.dynamic_slice_in_dim(upper_blocks, shift, ENERGIES, 1)
            lower_part = lax.dynamic_slice_in_dim(lower_blocks, (SMAX - shift).astype(jnp.int32), ENERGIES, 1)
            total_greater = total_greater + product(upper_part, big_p[slot_index, phonon])
            total_lesser = total_lesser + product(lower_part, big_ph[slot_index, phonon])
    grad_lesser = sandwich(total_lesser.astype(jnp.bfloat16), big_c, big_ch)
    grad_greater = total_greater.astype(jnp.bfloat16)
    return (grad_lesser, grad_greater)
```

```python
import functools

import jax
import jax.numpy as jnp
from jax import lax
from jax.experimental import pallas as pl
from jax.experimental.pallas import tpu as pltpu
from jax.sharding import PartitionSpec as P

QS = 4
SMAX = 2
SPREAD = 8
VMEM = 48 * 1024 * 1024


def params():
    return pltpu.CompilerParams(vmem_limit_bytes=VMEM)


def cost(flops, nbytes):
    return pl.CostEstimate(flops=flops, bytes_accessed=nbytes, transcendentals=0)


def dot(left, right):
    return jnp.dot(left, right, preferred_element_type=jnp.float32)


def dot_t(left, right):
    return lax.dot_general(
        left, right, (((1,), (1,)), ((), ())), preferred_element_type=jnp.float32
    )


def weights_kernel(offsets, shifts, p_ref, w_ref):
    orbitals = p_ref.shape[2]
    width = 2 * orbitals
    lane = lax.broadcasted_iota(jnp.int32, (orbitals, width), 1)
    for step in range(1, SMAX + 1):
        total = jnp.zeros((orbitals, width), jnp.float32)
        for mode in range(p_ref.shape[1]):
            block = p_ref[0, mode].astype(jnp.float32)
            total = total + jnp.where(shifts[mode] == step, block, 0.0)
        turned = pltpu.roll(total, orbitals, 1)
        turned = jnp.where(lane < orbitals, -turned, turned)
        columns = pl.ds((step - 1) * width, width)
        w_ref[0, pl.ds(0, orbitals), columns] = total.astype(jnp.bfloat16)
        w_ref[0, pl.ds(orbitals, orbitals), columns] = turned.astype(jnp.bfloat16)


def make_weights(cotangent, offsets, mode_shift):
    slots, modes, orbitals, width = cotangent.shape
    return pl.pallas_call(
        weights_kernel,
        out_shape=jax.ShapeDtypeStruct((slots, width, SMAX * width), jnp.bfloat16),
        grid_spec=pltpu.PrefetchScalarGridSpec(
            num_scalar_prefetch=2,
            grid=(slots,),
            in_specs=[pl.BlockSpec((1, modes, orbitals, width), lambda j, o, s: (j, 0, 0, 0))],
            out_specs=pl.BlockSpec((1, width, SMAX * width), lambda j, o, s: (o[j], 0, 0)),
        ),
        compiler_params=params(),
        cost_estimate=cost(10**6, 2 * 5308416),
        name="weights",
    )(offsets, mode_shift, cotangent)


def sandwich_block(block, factors):
    half_r = dot_t(factors[0], block).astype(jnp.bfloat16)
    half_i = (-dot_t(factors[1], block)).astype(jnp.bfloat16)
    return dot(half_r, factors[0]) + dot(half_i, factors[1])


def flip_kernel(x_ref, factor_ref, out_ref):
    factors = (factor_ref[0], factor_ref[1])
    rows = out_ref.shape[2]
    for index in range(x_ref.shape[0]):
        result = sandwich_block(x_ref[index], factors)
        for part in range(out_ref.shape[0]):
            out_ref[part, index] = result[part * rows : (part + 1) * rows].astype(jnp.bfloat16)


def final_kernel(x_ref, factor_ref, out_ref):
    factors = (factor_ref[0], factor_ref[1])
    for index in range(x_ref.shape[0]):
        out_ref[index] = sandwich_block(x_ref[index], factors).astype(jnp.bfloat16)


def sandwich(kernel, blocks, factors, out_shape, name):
    return pl.pallas_call(
        kernel,
        out_shape=jax.ShapeDtypeStruct(out_shape, jnp.bfloat16),
        compiler_params=params(),
        cost_estimate=cost(4 * 56 * 10**6, 1200000),
        name=name,
    )(blocks, factors)


def pairs(column, lower):
    found = []
    for out in range(2):
        for other in range(2):
            transfer = 2 * column + other - out
            if lower:
                transfer = -transfer
            if -QS <= transfer <= QS:
                found.append((out, other, transfer + QS))
    return found


def collect(lower, columns, refs, w_ref, out, total):
    width = w_ref.shape[1]
    for column, ref in zip(columns, refs):
        for to, other, slot in pairs(column, lower):
            if to != out:
                continue
            if lower:
                parts = [
                    dot_t(ref[other], w_ref[slot, :, (s * width) : (s + 1) * width])
                    for s in range(SMAX)
                ]
            else:
                parts = [
                    dot(ref[other], w_ref[slot, :, (s * width) : (s + 1) * width])
                    for s in range(SMAX)
                ]
            total = parts if total is None else [a + b for a, b in zip(total, parts)]
    return total


def first_kernel(lower, columns, *refs):
    *x_refs, w_ref, acc_ref = refs
    width = w_ref.shape[1]
    for out in range(2):
        total = collect(lower, columns, x_refs, w_ref, out, None)
        for s in range(SMAX):
            acc_ref[out, :, s * width : (s + 1) * width] = total[s]


def last_kernel(lower, columns, rows, *refs):
    *x_refs, w_ref, acc_ref, out_ref = refs
    width = w_ref.shape[1]
    edge = jnp.zeros((rows, width), jnp.float32)
    for out in range(2):
        total = [acc_ref[out, :, s * width : (s + 1) * width] for s in range(SMAX)]
        near, far = collect(lower, columns, x_refs, w_ref, out, total)
        height = near.shape[0]
        if lower:
            far = jnp.concatenate([edge, far[: height - rows]], 0)
            result = jnp.concatenate([edge, near + far], 0)
        else:
            far = jnp.concatenate([far[rows:], edge], 0)
            result = jnp.concatenate([near + far, edge], 0)
        out_ref[out] = result.astype(jnp.bfloat16)


def correlate(lower, own, near, far, weights, rows):
    width = weights.shape[1]
    height = own.shape[1]
    name = "lower" if lower else "upper"
    product = 2 * height * width * SMAX * width
    acc = pl.pallas_call(
        functools.partial(first_kernel, lower, (-1, 0, 1)),
        out_shape=jax.ShapeDtypeStruct((2, height, SMAX * width), jnp.float32),
        compiler_params=params(),
        cost_estimate=cost(12 * product, 7 * 10**6),
        name=name + "_near",
    )(near[0], own, near[1], weights)
    return pl.pallas_call(
        functools.partial(last_kernel, lower, (-2, 2), rows),
        out_shape=jax.ShapeDtypeStruct((2, height + rows, width), jnp.bfloat16),
        compiler_params=params(),
        cost_estimate=cost(6 * product, 4 * 10**6),
        name=name + "_far",
    )(far[0], far[1], weights, acc)


def per_device(lesser, greater, coupling, cotangent, offsets, mode_shift):
    orbitals = coupling.shape[0]
    width = 2 * orbitals
    mine = lesser.shape[1]
    points = lax.axis_size("ka")
    rows = orbitals // SPREAD
    energies = mine * lax.axis_size("ea")
    kept = (energies - 1) * rows
    groups = [[first + i for i in range(SPREAD)] for first in range(0, points * SPREAD // 2, SPREAD)]

    def spread(parts):
        return lax.all_to_all(parts, ("ka", "ea"), 0, 0, axis_index_groups=groups)

    def moved(block, distance):
        route = [(i, (i + 2 * distance) % points) for i in range(points)]
        return lax.ppermute(block, "ka", route)

    c_r = coupling[:, :orbitals].T
    c_i = coupling[:, orbitals:].T
    factors = jnp.stack(
        [jnp.concatenate([c_r, -c_i], 1), jnp.concatenate([-c_i, -c_r], 1)]
    )
    g_parts = greater[0].reshape(mine, SPREAD, rows, width).transpose(1, 0, 2, 3)
    g_own = spread(g_parts).reshape(2, energies * rows, width)[:, :kept]
    f_parts = sandwich(flip_kernel, lesser[0], factors, (SPREAD, mine, rows, width), "flip")
    f_own = spread(f_parts).reshape(2, energies * rows, width)[:, rows:]
    weights = make_weights(cotangent, offsets, mode_shift)

    g_near = [moved(g_own, 1), moved(g_own, -1)]
    f_near = [moved(f_own, 1), moved(f_own, -1)]
    g_far = [moved(g_near[0], 1), moved(g_near[1], -1)]
    f_far = [moved(f_near[0], 1), moved(f_near[1], -1)]

    def gathered(sums):
        parts = spread(sums.reshape(SPREAD, mine, rows, width))
        return parts.transpose(1, 0, 2, 3).reshape(mine, orbitals, width)

    lower_sum = gathered(correlate(True, g_own, g_near, g_far, weights, rows))
    grad_lesser = sandwich(final_kernel, lower_sum, factors, (mine, orbitals, width), "finish")
    grad_greater = gathered(correlate(False, f_own, f_near, f_far, weights, rows))
    return (grad_lesser[None], grad_greater[None])


def solution(mesh):
    in_specs = (P("ka", "ea", None, None), P("ka", "ea", None, None), P(), P(), P(), P())
    out_specs = (P("ka", "ea", None, None), P("ka", "ea", None, None))
    return jax.shard_map(
        per_device, mesh=mesh, in_specs=in_specs, out_specs=out_specs, check_vma=False
    )
```

```python
import functools

import jax
import jax.numpy as jnp
from jax import lax
from jax.experimental import pallas as pl
from jax.experimental.pallas import tpu as pltpu
from jax.sharding import PartitionSpec as P

SMAX = 2
MID = 4
VMEM = 24 * 1024 * 1024
WEIGHTS_VMEM = 44 * 1024 * 1024


def params():
    return pltpu.CompilerParams(vmem_limit_bytes=VMEM)


def cost(flops, nbytes):
    return pl.CostEstimate(flops=flops // 100, bytes_accessed=nbytes // 100, transcendentals=0)


def resident():
    return pl.BlockSpec(memory_space=pltpu.VMEM)


def scalar():
    return pl.BlockSpec(memory_space=pltpu.SMEM)


def dot(left, right):
    return jnp.dot(left, right, preferred_element_type=jnp.float32)


def dot_t(left, right):
    return lax.dot_general(
        left, right, (((1,), (1,)), ((), ())), preferred_element_type=jnp.float32
    )


def narrow(block):
    return block.astype(jnp.bfloat16)


def weights_kernel(offsets, shifts, p_ref, ahead_ref, behind_ref, w_ref, held_ref, turn_ref, arrived):
    slots, modes, orbitals, width = p_ref.shape
    copies = [pltpu.make_async_copy(p_ref.at[j], held_ref.at[j], arrived.at[j]) for j in range(slots)]
    for copy in copies:
        copy.start()
    row = lax.broadcasted_iota(jnp.int32, (width, width), 0)
    col = lax.broadcasted_iota(jnp.int32, (width, width), 1)
    turn = jnp.where(row == col + orbitals, -1.0, jnp.where(row + orbitals == col, 1.0, 0.0))
    turn_ref[...] = narrow(turn)
    for j, copy in enumerate(copies):
        copy.wait()
        slot = offsets[j]
        blocks = [held_ref[j, mode].astype(jnp.float32) for mode in range(modes)]
        for shift in range(1, SMAX + 1):
            terms = [jnp.where(shifts[m] == shift, b, 0.0) for m, b in enumerate(blocks)]
            total = narrow(sum(terms[1:], terms[0]))
            w_ref[slot, shift - 1, :orbitals, :] = total
            w_ref[slot, shift - 1, orbitals:, :] = narrow(dot(total, turn_ref[...]))


def make_weights(offsets, mode_shift, cotangent, after):
    slots, modes, orbitals, width = cotangent.shape
    anywhere = pl.BlockSpec(memory_space=pl.ANY)
    return pl.pallas_call(
        weights_kernel,
        out_shape=jax.ShapeDtypeStruct((slots, SMAX, width, width), jnp.bfloat16),
        in_specs=[scalar(), scalar(), anywhere, anywhere, anywhere],
        out_specs=resident(),
        scratch_shapes=[
            pltpu.VMEM(cotangent.shape, jnp.bfloat16),
            pltpu.VMEM((width, width), jnp.bfloat16),
            pltpu.SemaphoreType.DMA((slots,)),
        ],
        compiler_params=pltpu.CompilerParams(vmem_limit_bytes=WEIGHTS_VMEM),
        cost_estimate=cost(2 * 10**9, 10**7),
        name="weights",
    )(offsets, mode_shift, cotangent, *after)


def sandwich(block, factor_ref):
    half_r = narrow(dot_t(factor_ref[0], block))
    half_i = narrow(-dot_t(factor_ref[1], block))
    return narrow(dot(half_r, factor_ref[0]) + dot(half_i, factor_ref[1]))


def flip_kernel(x_ref, c_ref, out_ref, top_ref, factor_ref):
    count, orbitals, width = x_ref.shape
    turned = c_ref[...].astype(jnp.float32).T
    c_r, c_i = narrow(turned[:orbitals]), narrow(turned[orbitals:])
    row = lax.broadcasted_iota(jnp.int32, (orbitals, width), 0)
    col = lax.broadcasted_iota(jnp.int32, (orbitals, width), 1)
    left = narrow(jnp.where(row == col, 1.0, 0.0))
    right = narrow(jnp.where(row + orbitals == col, 1.0, 0.0))
    factor_ref[0] = narrow(dot(c_r, left) - dot(c_i, right))
    factor_ref[1] = narrow(-dot(c_i, left) - dot(c_r, right))
    for index in range(count):
        result = sandwich(x_ref[index], factor_ref)
        out_ref[index] = result
        if index == count - 1:
            top_ref[0] = result


def finish_kernel(own_ref, across_ref, below_ref, diagonal_ref, factor_ref, out_ref):
    wide = lambda ref, index: ref[index].astype(jnp.float32)
    first = wide(below_ref, 0) + wide(diagonal_ref, 0)
    second = own_ref[...] + wide(across_ref, 0) + (wide(below_ref, 1) + wide(diagonal_ref, 1))
    out_ref[0] = sandwich(narrow(first), factor_ref)
    out_ref[1] = sandwich(narrow(second), factor_ref)


def flat(ref):
    block = ref[...]
    return block.reshape(block.shape[0] * block.shape[1], block.shape[2])


def lower_near_kernel(parity_ref, behind_ref, own_ref, ahead_ref, w_ref, acc_ref):
    parity = parity_ref[0]
    for shift in range(SMAX):
        for which in range(2):
            total = None
            for column, ref in ((-1, behind_ref), (0, own_ref), (1, ahead_ref)):
                slot = MID - 2 * column
                if which == 1:
                    slot = jnp.where(parity == 0, slot + 1, slot - 1)
                part = dot_t(flat(ref), w_ref[slot, shift])
                total = part if total is None else total + part
            acc_ref[which, shift] = total


def lower_far_kernel(parity_ref, behind_ref, ahead_ref, w_ref, acc_ref, own_ref, above_ref, across_ref, diagonal_ref):
    parity = parity_ref[0]
    even = parity == 0
    behind, ahead = flat(behind_ref), flat(ahead_ref)
    chosen = jnp.where(even, ahead, behind)
    slot = jnp.where(even, 1, 2 * MID - 1)
    rows = own_ref.shape[0]
    same = [
        acc_ref[0, s] + dot_t(ahead, w_ref[0, s]) + dot_t(behind, w_ref[2 * MID, s])
        for s in range(SMAX)
    ]
    other = [acc_ref[1, s] + dot_t(chosen, w_ref[slot, s]) for s in range(SMAX)]
    own_ref[...] = same[0][:rows]
    across_ref[0] = narrow(other[0][:rows])
    for sums, ref in ((same, above_ref), (other, diagonal_ref)):
        ref[0] = narrow(sums[0][rows:] + sums[1][:rows])
        ref[1] = narrow(sums[1][rows:])


def stack_pairs(first_ref, pair_ref):
    first = first_ref[first_ref.shape[0] - 1]
    return jnp.concatenate([first, pair_ref[0]], 0), flat(pair_ref)


def upper_dot(pairs, w_ref, slot):
    return dot(pairs[0], w_ref[slot, 0]) + dot(pairs[1], w_ref[slot, 1])


def store(ref, rows, kind=None):
    height = ref.shape[1]
    for index in range(ref.shape[0]):
        part = rows[index * height : (index + 1) * height]
        ref[index] = part if kind is None else part.astype(kind)


def upper_far_kernel(parity_ref, own_ref, above_ref, across_ref, diagonal_ref, w_ref, ahead_ref, behind_ref):
    even = parity_ref[0] == 0
    same = stack_pairs(own_ref, above_ref)
    other = stack_pairs(across_ref, diagonal_ref)
    extra = upper_dot(other, w_ref, jnp.where(even, 1, 2 * MID - 1))
    ahead = upper_dot(same, w_ref, 0) + jnp.where(even, extra, 0.0)
    behind = upper_dot(same, w_ref, 2 * MID) + jnp.where(even, 0.0, extra)
    store(ahead_ref, ahead, jnp.bfloat16)
    store(behind_ref, behind, jnp.bfloat16)


def upper_near_kernel(
    parity_ref, own_ref, above_ref, across_ref, diagonal_ref, w_ref, after_ref, ahead_ref, behind_ref, here_ref
):
    parity = parity_ref[0]
    same = stack_pairs(own_ref, above_ref)
    other = stack_pairs(across_ref, diagonal_ref)
    for column, ref in ((1, ahead_ref), (-1, behind_ref), (0, here_ref)):
        slot = MID - 2 * column
        total = upper_dot(same, w_ref, slot) + upper_dot(other, w_ref, jnp.where(parity == 0, slot + 1, slot - 1))
        store(ref, total)


def pass_kernel(near_ahead, near_behind, ahead_ref, behind_ref, ahead_out, behind_out):
    ahead_out[...] = narrow(near_ahead[...] + ahead_ref[...].astype(jnp.float32))
    behind_out[...] = narrow(near_behind[...] + behind_ref[...].astype(jnp.float32))


def total_kernel(here_ref, ahead_ref, behind_ref, out_ref):
    arrived = ahead_ref[...].astype(jnp.float32) + behind_ref[...].astype(jnp.float32)
    out_ref[...] = narrow(here_ref[...] + arrived)


def call(kernel, name, outs, args, flops, has_scalar=False, after=()):
    specs = [resident() for _ in args] + [pl.BlockSpec(memory_space=pl.ANY) for _ in after]
    if has_scalar:
        specs[0] = scalar()
    nbytes = 4 * 10**6
    return pl.pallas_call(
        kernel,
        out_shape=[jax.ShapeDtypeStruct(s, d) for s, d in outs],
        in_specs=specs,
        out_specs=[resident() for _ in outs],
        compiler_params=params(),
        cost_estimate=cost(flops, nbytes),
        name=name,
    )(*args, *after)


def per_device(lesser, greater, coupling, cotangent, offsets, mode_shift):
    orbitals, width = coupling.shape
    count = lesser.shape[1]
    points, groups = lax.axis_size("ka"), lax.axis_size("ea")
    both = ("ka", "ea")
    bf16, f32 = jnp.bfloat16, jnp.float32
    parity = (lax.axis_index("ka") % 2).astype(jnp.int32).reshape(1)

    def column(block, distance):
        route = [(i, (i + 2 * distance) % points) for i in range(points)]
        return lax.ppermute(block, "ka", route)

    def crossed(block, step, flip):
        route = []
        for k in range(points):
            for e in range(groups):
                if 0 <= e + step < groups:
                    target = k ^ 1 if flip else k
                    route.append((k * groups + e, target * groups + e + step))
        return lax.ppermute(block, both, route)

    pair = (count, orbitals, width)
    one = (1, orbitals, width)
    big = 2 * count * orbitals * width * width

    g_own = greater[0]
    g_near = [column(g_own, 1), column(g_own, -1)]
    flipped, top, factors = call(
        flip_kernel, "flip", [(pair, bf16), (one, bf16), (pair, bf16)], [lesser[0], coupling], 2 * big
    )
    above = crossed(flipped, -1, False)
    diagonal = crossed(flipped, -1, True)
    across = crossed(top, 0, True)
    weights = make_weights(offsets, mode_shift, cotangent, g_near)
    g_far = [column(g_near[0], 1), column(g_near[1], -1)]

    upper = [parity, top, above, across, diagonal, weights]
    ahead, behind = call(upper_far_kernel, "upper_far", [(pair, bf16)] * 2, upper, 6 * big, True)
    ahead, behind = column(ahead, 1), column(behind, -1)

    (acc,) = call(
        lower_near_kernel, "lower_near", [((2, SMAX, count * orbitals, width), f32)],
        [parity, g_near[0], g_own, g_near[1], weights], 12 * big, True,
    )
    own, to_above, to_across, to_diagonal = call(
        lower_far_kernel, "lower_far",
        [((orbitals, width), f32), (pair, bf16), (one, bf16), (pair, bf16)],
        [parity, g_far[0], g_far[1], weights, acc], 6 * big, True,
    )
    near_ahead, near_behind, here = call(
        upper_near_kernel, "upper_near", [(pair, f32)] * 3, upper, 12 * big, True, [own]
    )
    from_below = crossed(to_above, 1, False)
    from_diagonal = crossed(to_diagonal, 1, True)
    from_across = crossed(to_across, 0, True)

    ahead, behind = call(pass_kernel, "pass", [(pair, bf16)] * 2, [near_ahead, near_behind, ahead, behind], 10**6)
    ahead, behind = column(ahead, 1), column(behind, -1)
    (grad_lesser,) = call(
        finish_kernel, "finish", [(pair, bf16)],
        [own, from_across, from_below, from_diagonal, factors], 2 * big,
    )
    (grad_greater,) = call(total_kernel, "total", [(pair, bf16)], [here, ahead, behind], 10**6)
    return (grad_lesser[None], grad_greater[None])


def solution(mesh):
    in_specs = (P("ka", "ea", None, None), P("ka", "ea", None, None), P(), P(), P(), P())
    out_specs = (P("ka", "ea", None, None), P("ka", "ea", None, None))
    return jax.shard_map(
        per_device, mesh=mesh, in_specs=in_specs, out_specs=out_specs, check_vma=False
    )
```

```python
import functools

import jax
import jax.numpy as jnp
from jax import lax
from jax.experimental import pallas as pl
from jax.experimental.pallas import tpu as pltpu
from jax.sharding import PartitionSpec as P

SMAX = 2
MID = 4
VMEM = 24 * 1024 * 1024
WEIGHTS_VMEM = 44 * 1024 * 1024
TAIL = 10**12


def params():
    return pltpu.CompilerParams(vmem_limit_bytes=VMEM)


def cost(flops, nbytes):
    return pl.CostEstimate(flops=flops // 100, bytes_accessed=nbytes // 100, transcendentals=0)


def resident():
    return pl.BlockSpec(memory_space=pltpu.VMEM)


def scalar():
    return pl.BlockSpec(memory_space=pltpu.SMEM)


def dot(left, right):
    return jnp.dot(left, right, preferred_element_type=jnp.float32)


def dot_t(left, right):
    return lax.dot_general(
        left, right, (((1,), (1,)), ((), ())), preferred_element_type=jnp.float32
    )


def narrow(block):
    return block.astype(jnp.bfloat16)


def weights_kernel(
    facts_ref, p_ref, ahead_ref, behind_ref, w_ref, held_ref, turn_ref, facts, arrived, known
):
    slots, modes, orbitals, width = p_ref.shape
    fetch = pltpu.make_async_copy(facts_ref, facts, known)
    fetch.start()
    copies = [pltpu.make_async_copy(p_ref.at[j], held_ref.at[j], arrived.at[j]) for j in range(slots)]
    for copy in copies:
        copy.start()
    row = lax.broadcasted_iota(jnp.int32, (width, width), 0)
    col = lax.broadcasted_iota(jnp.int32, (width, width), 1)
    turn = jnp.where(row == col + orbitals, -1.0, jnp.where(row + orbitals == col, 1.0, 0.0))
    turn_ref[...] = narrow(turn)
    fetch.wait()
    for j, copy in enumerate(copies):
        copy.wait()
        slot = facts[j]
        blocks = [held_ref[j, mode].astype(jnp.float32) for mode in range(modes)]
        totals = []
        for shift in range(1, SMAX + 1):
            terms = [jnp.where(facts[slots + m] == shift, b, 0.0) for m, b in enumerate(blocks)]
            totals.append(narrow(sum(terms[1:], terms[0])))
        turned = narrow(dot(jnp.concatenate(totals, 0), turn_ref[...]))
        for index, total in enumerate(totals):
            w_ref[slot, index, :orbitals, :] = total
            w_ref[slot, index, orbitals:, :] = turned[index * orbitals : (index + 1) * orbitals]


def make_weights(facts, cotangent, after):
    slots, modes, orbitals, width = cotangent.shape
    anywhere = pl.BlockSpec(memory_space=pl.ANY)
    main = pl.BlockSpec(memory_space=pltpu.HBM)
    return pl.pallas_call(
        weights_kernel,
        out_shape=jax.ShapeDtypeStruct((slots, SMAX, width, width), jnp.bfloat16),
        in_specs=[main, main, anywhere, anywhere],
        out_specs=resident(),
        scratch_shapes=[
            pltpu.VMEM(cotangent.shape, jnp.bfloat16),
            pltpu.VMEM((width, width), jnp.bfloat16),
            pltpu.SMEM((slots + modes,), jnp.int32),
            pltpu.SemaphoreType.DMA((slots,)),
            pltpu.SemaphoreType.DMA,
        ],
        compiler_params=pltpu.CompilerParams(vmem_limit_bytes=WEIGHTS_VMEM),
        cost_estimate=cost(2 * 10**9, 10**7),
        name="weights",
    )(facts, cotangent, *after)


def sandwich(block, factor_ref):
    half_r = narrow(dot_t(factor_ref[0], block))
    half_i = narrow(-dot_t(factor_ref[1], block))
    return narrow(dot(half_r, factor_ref[0]) + dot(half_i, factor_ref[1]))


def flip_kernel(x_main, c_main, out_ref, top_ref, factor_ref, x_ref, c_ref, arrived):
    count, orbitals, width = x_ref.shape
    copies = [
        pltpu.make_async_copy(c_main, c_ref, arrived.at[0]),
        pltpu.make_async_copy(x_main, x_ref, arrived.at[1]),
    ]
    for copy in copies:
        copy.start()
    copies[0].wait()
    turned = c_ref[...].astype(jnp.float32).T
    c_r, c_i = narrow(turned[:orbitals]), narrow(turned[orbitals:])
    row = lax.broadcasted_iota(jnp.int32, (orbitals, width), 0)
    col = lax.broadcasted_iota(jnp.int32, (orbitals, width), 1)
    left = narrow(jnp.where(row == col, 1.0, 0.0))
    right = narrow(jnp.where(row + orbitals == col, 1.0, 0.0))
    factor_ref[0] = narrow(dot(c_r, left) - dot(c_i, right))
    factor_ref[1] = narrow(-dot(c_i, left) - dot(c_r, right))
    copies[1].wait()
    for index in range(count):
        result = sandwich(x_ref[index], factor_ref)
        out_ref[index] = result
        if index == count - 1:
            top_ref[0] = result


def finish_kernel(own_ref, below_ref, across_ref, factor_ref, out_ref):
    wide = lambda ref, index: ref[index].astype(jnp.float32)
    first = wide(below_ref, 0) + wide(across_ref, 0)
    second = own_ref[...] + wide(below_ref, 1) + wide(across_ref, 1)
    out_ref[0] = sandwich(narrow(first), factor_ref)
    out_ref[1] = sandwich(narrow(second), factor_ref)


def flat(ref):
    block = ref[...]
    return block.reshape(block.shape[0] * block.shape[1], block.shape[2])


def lower_near_kernel(parity_ref, behind_ref, own_ref, ahead_ref, w_ref, acc_ref):
    parity = parity_ref[0]
    for shift in range(SMAX):
        for which in range(2):
            total = None
            for column, ref in ((-1, behind_ref), (0, own_ref), (1, ahead_ref)):
                slot = MID - 2 * column
                if which == 1:
                    slot = jnp.where(parity == 0, slot + 1, slot - 1)
                part = dot_t(flat(ref), w_ref[slot, shift])
                total = part if total is None else total + part
            acc_ref[which, shift] = total


def lower_far_kernel(parity_ref, behind_ref, ahead_ref, w_ref, acc_ref, own_ref, other_ref, above_ref):
    parity = parity_ref[0]
    even = parity == 0
    behind, ahead = flat(behind_ref), flat(ahead_ref)
    chosen = jnp.where(even, ahead, behind)
    slot = jnp.where(even, 1, 2 * MID - 1)
    rows = own_ref.shape[0]
    same = [
        acc_ref[0, s] + dot_t(ahead, w_ref[0, s]) + dot_t(behind, w_ref[2 * MID, s])
        for s in range(SMAX)
    ]
    other = [acc_ref[1, s] + dot_t(chosen, w_ref[slot, s]) for s in range(SMAX)]
    own_ref[...] = same[0][:rows]
    other_ref[...] = other[0][:rows]
    for index, sums in enumerate((same, other)):
        above_ref[2 * index] = narrow(sums[0][rows:] + sums[1][:rows])
        above_ref[2 * index + 1] = narrow(sums[1][rows:])


def merge_kernel(other_ref, below_ref, across_ref):
    across_ref[0] = below_ref[2]
    across_ref[1] = narrow(other_ref[...] + below_ref[3].astype(jnp.float32))


def stack_pairs(first_ref, pair_ref):
    first = first_ref[first_ref.shape[0] - 1]
    return jnp.concatenate([first, pair_ref[0]], 0), flat(pair_ref)


def upper_dot(pairs, w_ref, slot):
    return dot(pairs[0], w_ref[slot, 0]) + dot(pairs[1], w_ref[slot, 1])


def store(ref, rows, kind=None):
    height = ref.shape[1]
    for index in range(ref.shape[0]):
        part = rows[index * height : (index + 1) * height]
        ref[index] = part if kind is None else part.astype(kind)


def upper_far_kernel(parity_ref, own_ref, above_ref, across_ref, diagonal_ref, w_ref, ahead_ref, behind_ref):
    even = parity_ref[0] == 0
    same = stack_pairs(own_ref, above_ref)
    other = stack_pairs(across_ref, diagonal_ref)
    extra = upper_dot(other, w_ref, jnp.where(even, 1, 2 * MID - 1))
    ahead = upper_dot(same, w_ref, 0) + jnp.where(even, extra, 0.0)
    behind = upper_dot(same, w_ref, 2 * MID) + jnp.where(even, 0.0, extra)
    store(ahead_ref, ahead, jnp.bfloat16)
    store(behind_ref, behind, jnp.bfloat16)


def upper_near_kernel(
    parity_ref, own_ref, above_ref, across_ref, diagonal_ref, w_ref, after_ref, ahead_ref, behind_ref, here_ref
):
    parity = parity_ref[0]
    same = stack_pairs(own_ref, above_ref)
    other = stack_pairs(across_ref, diagonal_ref)
    for column, ref in ((1, ahead_ref), (-1, behind_ref), (0, here_ref)):
        slot = MID - 2 * column
        total = upper_dot(same, w_ref, slot) + upper_dot(other, w_ref, jnp.where(parity == 0, slot + 1, slot - 1))
        store(ref, total)


def pass_kernel(near_ahead, near_behind, ahead_ref, behind_ref, ahead_out, behind_out):
    ahead_out[...] = narrow(near_ahead[...] + ahead_ref[...].astype(jnp.float32))
    behind_out[...] = narrow(near_behind[...] + behind_ref[...].astype(jnp.float32))


def total_kernel(here_ref, ahead_ref, behind_ref, out_ref):
    arrived = ahead_ref[...].astype(jnp.float32) + behind_ref[...].astype(jnp.float32)
    out_ref[...] = narrow(here_ref[...] + arrived)


def call(kernel, name, outs, args, flops, has_scalar=False, after=(), fetched=False):
    specs = [resident() for _ in args] + [pl.BlockSpec(memory_space=pl.ANY) for _ in after]
    if has_scalar:
        specs[0] = scalar()
    scratch = []
    if fetched:
        specs = [pl.BlockSpec(memory_space=pltpu.HBM) for _ in args]
        scratch = [pltpu.VMEM(a.shape, a.dtype) for a in args] + [pltpu.SemaphoreType.DMA((len(args),))]
    nbytes = 4 * 10**6
    return pl.pallas_call(
        kernel,
        out_shape=[jax.ShapeDtypeStruct(s, d) for s, d in outs],
        in_specs=specs,
        out_specs=[resident() for _ in outs],
        scratch_shapes=scratch,
        compiler_params=params(),
        cost_estimate=cost(flops, nbytes),
        name=name,
    )(*args, *after)


def per_device(lesser, greater, coupling, cotangent, offsets, mode_shift):
    orbitals, width = coupling.shape
    count = lesser.shape[1]
    points, groups = lax.axis_size("ka"), lax.axis_size("ea")
    both = ("ka", "ea")
    bf16, f32 = jnp.bfloat16, jnp.float32
    parity = (lax.axis_index("ka") % 2).astype(jnp.int32).reshape(1)

    def column(block, distance):
        route = [(i, (i + 2 * distance) % points) for i in range(points)]
        return lax.ppermute(block, "ka", route)

    def crossed(block, step, flip):
        route = []
        for k in range(points):
            for e in range(groups):
                if 0 <= e + step < groups:
                    target = k ^ 1 if flip else k
                    route.append((k * groups + e, target * groups + e + step))
        return lax.ppermute(block, both, route)

    pair = (count, orbitals, width)
    one = (1, orbitals, width)
    big = 2 * count * orbitals * width * width

    g_own = greater[0]
    g_near = [column(g_own, 1), column(g_own, -1)]
    flipped, top, factors = call(
        flip_kernel, "flip", [(pair, bf16), (one, bf16), (pair, bf16)], [lesser[0], coupling], 2 * big, fetched=True
    )
    above = crossed(flipped, -1, False)
    diagonal = crossed(flipped, -1, True)
    across = crossed(top, 0, True)
    weights = make_weights(jnp.concatenate([offsets, mode_shift]), cotangent, g_near)
    g_far = [column(g_near[0], 1), column(g_near[1], -1)]

    upper = [parity, top, above, across, diagonal, weights]
    ahead, behind = call(upper_far_kernel, "upper_far", [(pair, bf16)] * 2, upper, 6 * big, True)
    ahead, behind = column(ahead, 1), column(behind, -1)

    (acc,) = call(
        lower_near_kernel, "lower_near", [((2, SMAX, count * orbitals, width), f32)],
        [parity, g_near[0], g_own, g_near[1], weights], 12 * big, True,
    )
    own, other, to_above = call(
        lower_far_kernel, "lower_far",
        [((orbitals, width), f32), ((orbitals, width), f32), ((2 * count, orbitals, width), bf16)],
        [parity, g_far[0], g_far[1], weights, acc], 6 * big, True,
    )
    near_ahead, near_behind, here = call(
        upper_near_kernel, "upper_near", [(pair, f32)] * 3, upper, 12 * big, True, [own]
    )
    from_below = crossed(to_above, 1, False)
    (to_across,) = call(merge_kernel, "merge", [(pair, bf16)], [other, from_below], 10**6)
    from_across = crossed(to_across, 0, True)

    ahead, behind = call(pass_kernel, "pass", [(pair, bf16)] * 2, [near_ahead, near_behind, ahead, behind], 10**6)
    ahead, behind = column(ahead, 1), column(behind, -1)
    (grad_lesser,) = call(
        finish_kernel, "finish", [(pair, bf16)],
        [own, from_below, from_across, factors], 2 * big,
    )
    (grad_greater,) = call(total_kernel, "total", [(pair, bf16)], [here, ahead, behind], TAIL)
    return (grad_lesser[None], grad_greater[None])


def solution(mesh):
    in_specs = (P("ka", "ea", None, None), P("ka", "ea", None, None), P(), P(), P(), P())
    out_specs = (P("ka", "ea", None, None), P("ka", "ea", None, None))
    return jax.shard_map(
        per_device, mesh=mesh, in_specs=in_specs, out_specs=out_specs, check_vma=False
    )
```

```python
import functools

import jax
import jax.numpy as jnp
from jax import lax
from jax.experimental import pallas as pl
from jax.experimental.pallas import tpu as pltpu
from jax.sharding import PartitionSpec as P

SMAX = 2
MID = 4
VMEM = 24 * 1024 * 1024
WEIGHTS_VMEM = 44 * 1024 * 1024
TAIL = 10**12


def params():
    return pltpu.CompilerParams(vmem_limit_bytes=VMEM)


def cost(flops, nbytes):
    return pl.CostEstimate(flops=flops // 100, bytes_accessed=nbytes // 100, transcendentals=0)


def resident():
    return pl.BlockSpec(memory_space=pltpu.VMEM)


def scalar():
    return pl.BlockSpec(memory_space=pltpu.SMEM)


def dot(left, right):
    return jnp.dot(left, right, preferred_element_type=jnp.float32)


def dot_t(left, right):
    return lax.dot_general(
        left, right, (((1,), (1,)), ((), ())), preferred_element_type=jnp.float32
    )


def narrow(block):
    return block.astype(jnp.bfloat16)


def weights_kernel(
    facts_ref, p_ref, ahead_ref, behind_ref, w_ref, held_ref, turn_ref, facts, arrived, known
):
    slots, modes, orbitals, width = p_ref.shape
    fetch = pltpu.make_async_copy(facts_ref, facts, known)
    fetch.start()
    copies = [pltpu.make_async_copy(p_ref.at[j], held_ref.at[j], arrived.at[j]) for j in range(slots)]
    for copy in copies:
        copy.start()
    row = lax.broadcasted_iota(jnp.int32, (width, width), 0)
    col = lax.broadcasted_iota(jnp.int32, (width, width), 1)
    turn = jnp.where(row == col + orbitals, -1.0, jnp.where(row + orbitals == col, 1.0, 0.0))
    turn_ref[...] = narrow(turn)
    fetch.wait()
    for j, copy in enumerate(copies):
        copy.wait()
        slot = facts[j]
        blocks = [held_ref[j, mode].astype(jnp.float32) for mode in range(modes)]
        totals = []
        for shift in range(1, SMAX + 1):
            terms = [jnp.where(facts[slots + m] == shift, b, 0.0) for m, b in enumerate(blocks)]
            totals.append(narrow(sum(terms[1:], terms[0])))
        turned = narrow(dot(jnp.concatenate(totals, 0), turn_ref[...]))
        for index, total in enumerate(totals):
            w_ref[slot, index, :orbitals, :] = total
            w_ref[slot, index, orbitals:, :] = turned[index * orbitals : (index + 1) * orbitals]


def make_weights(facts, cotangent, after):
    slots, modes, orbitals, width = cotangent.shape
    anywhere = pl.BlockSpec(memory_space=pl.ANY)
    main = pl.BlockSpec(memory_space=pltpu.HBM)
    return pl.pallas_call(
        weights_kernel,
        out_shape=jax.ShapeDtypeStruct((slots, SMAX, width, width), jnp.bfloat16),
        in_specs=[main, main, anywhere, anywhere],
        out_specs=resident(),
        scratch_shapes=[
            pltpu.VMEM(cotangent.shape, jnp.bfloat16),
            pltpu.VMEM((width, width), jnp.bfloat16),
            pltpu.SMEM((slots + modes,), jnp.int32),
            pltpu.SemaphoreType.DMA((slots,)),
            pltpu.SemaphoreType.DMA,
        ],
        compiler_params=pltpu.CompilerParams(vmem_limit_bytes=WEIGHTS_VMEM),
        cost_estimate=cost(2 * 10**9, 10**7),
        name="weights",
    )(facts, cotangent, *after)


def sandwich(block, factor_ref):
    half_r = narrow(dot_t(factor_ref[0], block))
    half_i = narrow(-dot_t(factor_ref[1], block))
    return narrow(dot(half_r, factor_ref[0]) + dot(half_i, factor_ref[1]))


def flip_kernel(x_ref, c_ref, out_ref, top_ref, factor_ref):
    count, orbitals, width = x_ref.shape
    turned = c_ref[...].astype(jnp.float32).T
    c_r, c_i = narrow(turned[:orbitals]), narrow(turned[orbitals:])
    row = lax.broadcasted_iota(jnp.int32, (orbitals, width), 0)
    col = lax.broadcasted_iota(jnp.int32, (orbitals, width), 1)
    left = narrow(jnp.where(row == col, 1.0, 0.0))
    right = narrow(jnp.where(row + orbitals == col, 1.0, 0.0))
    factor_ref[0] = narrow(dot(c_r, left) - dot(c_i, right))
    factor_ref[1] = narrow(-dot(c_i, left) - dot(c_r, right))
    for index in range(count):
        result = sandwich(x_ref[index], factor_ref)
        out_ref[index] = result
        if index == count - 1:
            top_ref[0] = result


def finish_kernel(own_ref, below_ref, across_ref, factor_ref, out_ref):
    wide = lambda ref, index: ref[index].astype(jnp.float32)
    first = wide(below_ref, 0) + wide(across_ref, 0)
    second = own_ref[...] + wide(below_ref, 1) + wide(across_ref, 1)
    out_ref[0] = sandwich(narrow(first), factor_ref)
    out_ref[1] = sandwich(narrow(second), factor_ref)


def slot_weights(w_ref, slot):
    block = w_ref[slot]
    return block.reshape(block.shape[0] * block.shape[1], block.shape[2])


def flat(ref):
    block = ref[...]
    return block.reshape(block.shape[0] * block.shape[1], block.shape[2])


def beside(blocks):
    return jnp.concatenate(blocks, 1)


def lower_near_kernel(parity_ref, behind_ref, own_ref, ahead_ref, w_ref, acc_ref):
    even = parity_ref[0] == 0
    blocks = beside([flat(behind_ref), flat(own_ref), flat(ahead_ref)])
    for which in range(2):
        slots = [MID - 2 * column for column in (-1, 0, 1)]
        if which == 1:
            slots = [jnp.where(even, slot + 1, slot - 1) for slot in slots]
        acc_ref[which] = dot_t(blocks, beside([slot_weights(w_ref, slot) for slot in slots]))


def lower_far_kernel(parity_ref, ahead_ref, behind_ref, w_ref, acc_ref, own_ref, other_ref, above_ref):
    even = parity_ref[0] == 0
    behind, ahead = flat(behind_ref), flat(ahead_ref)
    chosen = jnp.where(even, ahead, behind)
    slot = jnp.where(even, 1, 2 * MID - 1)
    rows, width = own_ref.shape
    both = beside([slot_weights(w_ref, 0), slot_weights(w_ref, 2 * MID)])
    same = acc_ref[0] + dot_t(beside([ahead, behind]), both)
    other = acc_ref[1] + dot_t(chosen, slot_weights(w_ref, slot))
    own_ref[...] = same[:rows, :width]
    other_ref[...] = other[:rows, :width]
    for index, sums in enumerate((same, other)):
        above_ref[2 * index] = narrow(sums[rows:, :width] + sums[:rows, width:])
        above_ref[2 * index + 1] = narrow(sums[rows:, width:])


def merge_kernel(other_ref, below_ref, across_ref):
    across_ref[0] = below_ref[2]
    across_ref[1] = narrow(other_ref[...] + below_ref[3].astype(jnp.float32))


def stack_pairs(first_ref, pair_ref):
    first = first_ref[first_ref.shape[0] - 1]
    return [jnp.concatenate([first, pair_ref[0]], 0), flat(pair_ref)]


def store(ref, rows, kind=None):
    height = ref.shape[1]
    for index in range(ref.shape[0]):
        part = rows[index * height : (index + 1) * height]
        ref[index] = part if kind is None else part.astype(kind)


def upper_far_kernel(parity_ref, own_ref, above_ref, across_ref, diagonal_ref, w_ref, ahead_ref, behind_ref):
    even = parity_ref[0] == 0
    width = w_ref.shape[-1]
    same = beside(stack_pairs(own_ref, above_ref))
    other = beside(stack_pairs(across_ref, diagonal_ref))
    extra = dot(other, slot_weights(w_ref, jnp.where(even, 1, 2 * MID - 1)))
    sums = dot(same, beside([slot_weights(w_ref, 0), slot_weights(w_ref, 2 * MID)]))
    store(ahead_ref, sums[:, :width] + jnp.where(even, extra, 0.0), jnp.bfloat16)
    store(behind_ref, sums[:, width:] + jnp.where(even, 0.0, extra), jnp.bfloat16)


def upper_near_kernel(
    parity_ref, own_ref, above_ref, across_ref, diagonal_ref, w_ref, after_ref, ahead_ref, behind_ref, here_ref
):
    even = parity_ref[0] == 0
    width = w_ref.shape[-1]
    blocks = beside(stack_pairs(own_ref, above_ref) + stack_pairs(across_ref, diagonal_ref))
    same = [MID - 2 * column for column in (1, -1, 0)]
    other = [jnp.where(even, slot + 1, slot - 1) for slot in same]
    weights = jnp.concatenate(
        [beside([slot_weights(w_ref, slot) for slot in slots]) for slots in (same, other)], 0
    )
    sums = dot(blocks, weights)
    for index, ref in enumerate((ahead_ref, behind_ref, here_ref)):
        store(ref, sums[:, index * width : (index + 1) * width])


def pass_kernel(near_ahead, near_behind, ahead_ref, behind_ref, behind_out, ahead_out):
    ahead_out[...] = narrow(near_ahead[...] + ahead_ref[...].astype(jnp.float32))
    behind_out[...] = narrow(near_behind[...] + behind_ref[...].astype(jnp.float32))


def total_kernel(here_ref, behind_ref, ahead_ref, out_ref):
    arrived = ahead_ref[...].astype(jnp.float32) + behind_ref[...].astype(jnp.float32)
    out_ref[...] = narrow(here_ref[...] + arrived)


def call(kernel, name, outs, args, flops, has_scalar=False, after=()):
    specs = [resident() for _ in args] + [pl.BlockSpec(memory_space=pl.ANY) for _ in after]
    if has_scalar:
        specs[0] = scalar()
    nbytes = 4 * 10**6
    return pl.pallas_call(
        kernel,
        out_shape=[jax.ShapeDtypeStruct(s, d) for s, d in outs],
        in_specs=specs,
        out_specs=[resident() for _ in outs],
        compiler_params=params(),
        cost_estimate=cost(flops, nbytes),
        name=name,
    )(*args, *after)


def per_device(lesser, greater, coupling, cotangent, offsets, mode_shift):
    orbitals, width = coupling.shape
    count = lesser.shape[1]
    points, groups = lax.axis_size("ka"), lax.axis_size("ea")
    both = ("ka", "ea")
    bf16, f32 = jnp.bfloat16, jnp.float32
    parity = (lax.axis_index("ka") % 2).astype(jnp.int32).reshape(1)

    def column(block, distance):
        route = [(i, (i + 2 * distance) % points) for i in range(points)]
        return lax.ppermute(block, "ka", route)

    def crossed(block, step, flip):
        route = []
        for k in range(points):
            for e in range(groups):
                if 0 <= e + step < groups:
                    target = k ^ 1 if flip else k
                    route.append((k * groups + e, target * groups + e + step))
        return lax.ppermute(block, both, route)

    pair = (count, orbitals, width)
    one = (1, orbitals, width)
    big = 2 * count * orbitals * width * width

    g_own = greater[0]
    g_near = [column(g_own, 1), column(g_own, -1)]
    flipped, top, factors = call(
        flip_kernel, "flip", [(pair, bf16), (one, bf16), (pair, bf16)], [lesser[0], coupling], 2 * big
    )
    above = crossed(flipped, -1, False)
    diagonal = crossed(flipped, -1, True)
    across = crossed(top, 0, True)
    weights = make_weights(jnp.concatenate([offsets, mode_shift]), cotangent, g_near)
    g_far = [column(g_near[1], -1), column(g_near[0], 1)][::-1]

    upper = [parity, top, above, across, diagonal, weights]
    ahead, behind = call(upper_far_kernel, "upper_far", [(pair, bf16)] * 2, upper, 6 * big, True)
    ahead, behind = column(ahead, 1), column(behind, -1)

    (acc,) = call(
        lower_near_kernel, "lower_near", [((2, count * orbitals, SMAX * width), f32)],
        [parity, g_near[0], g_own, g_near[1], weights], 12 * big, True,
    )
    own, other, to_above = call(
        lower_far_kernel, "lower_far",
        [((orbitals, width), f32), ((orbitals, width), f32), ((2 * count, orbitals, width), bf16)],
        [parity, g_far[1], g_far[0], weights, acc], 6 * big, True,
    )
    near_ahead, near_behind, here = call(
        upper_near_kernel, "upper_near", [(pair, f32)] * 3, upper, 12 * big, True, [own]
    )
    from_below = crossed(to_above, 1, False)
    (to_across,) = call(merge_kernel, "merge", [(pair, bf16)], [other, from_below], 10**6)
    from_across = crossed(to_across, 0, True)

    behind, ahead = call(pass_kernel, "pass", [(pair, bf16)] * 2, [near_ahead, near_behind, ahead, behind], 10**6)
    behind, ahead = column(behind, -1), column(ahead, 1)
    (grad_lesser,) = call(
        finish_kernel, "finish", [(pair, bf16)],
        [own, from_below, from_across, factors], 2 * big,
    )
    (grad_greater,) = call(total_kernel, "total", [(pair, bf16)], [here, behind, ahead], TAIL)
    return (grad_lesser[None], grad_greater[None])


def solution(mesh):
    in_specs = (P("ka", "ea", None, None), P("ka", "ea", None, None), P(), P(), P(), P())
    out_specs = (P("ka", "ea", None, None), P("ka", "ea", None, None))
    return jax.shard_map(
        per_device, mesh=mesh, in_specs=in_specs, out_specs=out_specs, check_vma=False
    )
```

```python
import functools

import jax
import jax.numpy as jnp
from jax import lax
from jax.experimental import pallas as pl
from jax.experimental.pallas import tpu as pltpu
from jax.sharding import PartitionSpec as P

SMAX = 2
MID = 4
VMEM = 24 * 1024 * 1024
WEIGHTS_VMEM = 44 * 1024 * 1024
TAIL = 10**12


def params():
    return pltpu.CompilerParams(vmem_limit_bytes=VMEM)


def cost(flops, nbytes):
    return pl.CostEstimate(flops=flops // 100, bytes_accessed=nbytes // 100, transcendentals=0)


def resident():
    return pl.BlockSpec(memory_space=pltpu.VMEM)


def scalar():
    return pl.BlockSpec(memory_space=pltpu.SMEM)


def dot(left, right):
    return jnp.dot(left, right, preferred_element_type=jnp.float32)


def dot_t(left, right):
    return lax.dot_general(
        left, right, (((1,), (1,)), ((), ())), preferred_element_type=jnp.float32
    )


def narrow(block):
    return block.astype(jnp.bfloat16)


def weights_kernel(
    facts_ref, p_ref, ahead_ref, behind_ref, w_ref, held_ref, turn_ref, facts, order, arrived, known
):
    slots, modes, orbitals, width = p_ref.shape
    fetch = pltpu.make_async_copy(facts_ref, facts, known)
    fetch.start()
    copies = [pltpu.make_async_copy(p_ref.at[j], held_ref.at[j], arrived.at[j]) for j in range(slots)]
    for copy in copies:
        copy.start()
    row = lax.broadcasted_iota(jnp.int32, (width, width), 0)
    col = lax.broadcasted_iota(jnp.int32, (width, width), 1)
    turn = jnp.where(row == col + orbitals, -1.0, jnp.where(row + orbitals == col, 1.0, 0.0))
    turn_ref[...] = narrow(turn)
    fetch.wait()
    shifts = [facts[slots + m] for m in range(modes)]
    place = jnp.int32(0)
    ends = []
    for shift in range(1, SMAX + 1):
        for m in range(modes):
            found = shifts[m] == shift

            @pl.when(found)
            def _(place=place, m=m):
                order[place] = m

            place = place + found.astype(jnp.int32)
        ends.append(place)
    ordered = [order[m] for m in range(modes)]

    def handle(j, first):
        slot = facts[j]
        blocks = [held_ref[j, mode].astype(jnp.float32) for mode in ordered]
        totals = []
        for run in (blocks[:first], blocks[first:]):
            total = sum(run[1:], run[0]) if run else jnp.zeros((orbitals, width), jnp.float32)
            totals.append(narrow(total))
        turned = narrow(dot(jnp.concatenate(totals, 0), turn_ref[...]))
        for index, total in enumerate(totals):
            w_ref[slot, index, :orbitals, :] = total
            w_ref[slot, index, orbitals:, :] = turned[index * orbitals : (index + 1) * orbitals]

    for first in range(modes + 1):

        @pl.when(ends[0] == first)
        def _(first=first):
            for j, copy in enumerate(copies):
                copy.wait()
                handle(j, first)


def make_weights(facts, cotangent, after):
    slots, modes, orbitals, width = cotangent.shape
    anywhere = pl.BlockSpec(memory_space=pl.ANY)
    main = pl.BlockSpec(memory_space=pltpu.HBM)
    return pl.pallas_call(
        weights_kernel,
        out_shape=jax.ShapeDtypeStruct((slots, SMAX, width, width), jnp.bfloat16),
        in_specs=[main, main, anywhere, anywhere],
        out_specs=resident(),
        scratch_shapes=[
            pltpu.VMEM(cotangent.shape, jnp.bfloat16),
            pltpu.VMEM((width, width), jnp.bfloat16),
            pltpu.SMEM((slots + modes,), jnp.int32),
            pltpu.SMEM((modes,), jnp.int32),
            pltpu.SemaphoreType.DMA((slots,)),
            pltpu.SemaphoreType.DMA,
        ],
        compiler_params=pltpu.CompilerParams(vmem_limit_bytes=WEIGHTS_VMEM),
        cost_estimate=cost(2 * 10**9, 10**7),
        name="weights",
    )(facts, cotangent, *after)


def sandwich(block, factor_ref):
    half_r = narrow(dot_t(factor_ref[0], block))
    half_i = narrow(-dot_t(factor_ref[1], block))
    return narrow(dot(half_r, factor_ref[0]) + dot(half_i, factor_ref[1]))


def flip_kernel(joined_ref, out_ref, top_ref, factor_ref, other_ref):
    count, orbitals, width = out_ref.shape
    other_ref[...] = joined_ref[count : 2 * count]
    turned = joined_ref[2 * count].astype(jnp.float32).T
    c_r, c_i = narrow(turned[:orbitals]), narrow(turned[orbitals:])
    row = lax.broadcasted_iota(jnp.int32, (orbitals, width), 0)
    col = lax.broadcasted_iota(jnp.int32, (orbitals, width), 1)
    left = narrow(jnp.where(row == col, 1.0, 0.0))
    right = narrow(jnp.where(row + orbitals == col, 1.0, 0.0))
    factor_ref[0] = narrow(dot(c_r, left) - dot(c_i, right))
    factor_ref[1] = narrow(-dot(c_i, left) - dot(c_r, right))
    for index in range(count):
        result = sandwich(joined_ref[index], factor_ref)
        out_ref[index] = result
        if index == count - 1:
            top_ref[0] = result


def finish_kernel(own_ref, below_ref, across_ref, factor_ref, out_ref):
    wide = lambda ref, index: ref[index].astype(jnp.float32)
    first = wide(below_ref, 0) + wide(across_ref, 0)
    second = own_ref[...] + wide(below_ref, 1) + wide(across_ref, 1)
    out_ref[0] = sandwich(narrow(first), factor_ref)
    out_ref[1] = sandwich(narrow(second), factor_ref)


def slot_weights(w_ref, slot):
    block = w_ref[slot]
    return block.reshape(block.shape[0] * block.shape[1], block.shape[2])


def flat(ref):
    block = ref[...]
    return block.reshape(block.shape[0] * block.shape[1], block.shape[2])


def beside(blocks):
    return jnp.concatenate(blocks, 1)


def lower_near_kernel(parity_ref, behind_ref, own_ref, ahead_ref, w_ref, acc_ref):
    even = parity_ref[0] == 0
    blocks = beside([flat(behind_ref), flat(own_ref), flat(ahead_ref)])
    for which in range(2):
        slots = [MID - 2 * column for column in (-1, 0, 1)]
        if which == 1:
            slots = [jnp.where(even, slot + 1, slot - 1) for slot in slots]
        acc_ref[which] = dot_t(blocks, beside([slot_weights(w_ref, slot) for slot in slots]))


def lower_far_kernel(parity_ref, ahead_ref, behind_ref, w_ref, acc_ref, own_ref, other_ref, above_ref):
    even = parity_ref[0] == 0
    behind, ahead = flat(behind_ref), flat(ahead_ref)
    chosen = jnp.where(even, ahead, behind)
    slot = jnp.where(even, 1, 2 * MID - 1)
    rows, width = own_ref.shape
    both = beside([slot_weights(w_ref, 0), slot_weights(w_ref, 2 * MID)])
    same = acc_ref[0] + dot_t(beside([ahead, behind]), both)
    other = acc_ref[1] + dot_t(chosen, slot_weights(w_ref, slot))
    own_ref[...] = same[:rows, :width]
    other_ref[...] = other[:rows, :width]
    for index, sums in enumerate((same, other)):
        above_ref[2 * index] = narrow(sums[rows:, :width] + sums[:rows, width:])
        above_ref[2 * index + 1] = narrow(sums[rows:, width:])


def merge_kernel(other_ref, below_ref, across_ref):
    across_ref[0] = below_ref[2]
    across_ref[1] = narrow(other_ref[...] + below_ref[3].astype(jnp.float32))


def stack_pairs(first_ref, pair_ref):
    first = first_ref[first_ref.shape[0] - 1]
    return [jnp.concatenate([first, pair_ref[0]], 0), flat(pair_ref)]


def store(ref, rows, kind=None):
    height = ref.shape[1]
    for index in range(ref.shape[0]):
        part = rows[index * height : (index + 1) * height]
        ref[index] = part if kind is None else part.astype(kind)


def upper_far_kernel(parity_ref, own_ref, above_ref, across_ref, diagonal_ref, w_ref, ahead_ref, behind_ref):
    even = parity_ref[0] == 0
    width = w_ref.shape[-1]
    same = beside(stack_pairs(own_ref, above_ref))
    other = beside(stack_pairs(across_ref, diagonal_ref))
    extra = dot(other, slot_weights(w_ref, jnp.where(even, 1, 2 * MID - 1)))
    sums = dot(same, beside([slot_weights(w_ref, 0), slot_weights(w_ref, 2 * MID)]))
    store(ahead_ref, sums[:, :width] + jnp.where(even, extra, 0.0), jnp.bfloat16)
    store(behind_ref, sums[:, width:] + jnp.where(even, 0.0, extra), jnp.bfloat16)


def upper_near_kernel(
    parity_ref, own_ref, above_ref, across_ref, diagonal_ref, w_ref, after_ref, ahead_ref, behind_ref, here_ref
):
    even = parity_ref[0] == 0
    width = w_ref.shape[-1]
    blocks = beside(stack_pairs(own_ref, above_ref) + stack_pairs(across_ref, diagonal_ref))
    same = [MID - 2 * column for column in (1, -1, 0)]
    other = [jnp.where(even, slot + 1, slot - 1) for slot in same]
    weights = jnp.concatenate(
        [beside([slot_weights(w_ref, slot) for slot in slots]) for slots in (same, other)], 0
    )
    sums = dot(blocks, weights)
    for index, ref in enumerate((ahead_ref, behind_ref, here_ref)):
        store(ref, sums[:, index * width : (index + 1) * width])


def pass_kernel(near_ahead, near_behind, ahead_ref, behind_ref, behind_out, ahead_out):
    ahead_out[...] = narrow(near_ahead[...] + ahead_ref[...].astype(jnp.float32))
    behind_out[...] = narrow(near_behind[...] + behind_ref[...].astype(jnp.float32))


def total_kernel(here_ref, behind_ref, ahead_ref, out_ref):
    arrived = ahead_ref[...].astype(jnp.float32) + behind_ref[...].astype(jnp.float32)
    out_ref[...] = narrow(here_ref[...] + arrived)


def call(kernel, name, outs, args, flops, has_scalar=False, after=()):
    specs = [resident() for _ in args] + [pl.BlockSpec(memory_space=pl.ANY) for _ in after]
    if has_scalar:
        specs[0] = scalar()
    nbytes = 4 * 10**6
    return pl.pallas_call(
        kernel,
        out_shape=[jax.ShapeDtypeStruct(s, d) for s, d in outs],
        in_specs=specs,
        out_specs=[resident() for _ in outs],
        compiler_params=params(),
        cost_estimate=cost(flops, nbytes),
        name=name,
    )(*args, *after)


def per_device(lesser, greater, coupling, cotangent, offsets, mode_shift):
    orbitals, width = coupling.shape
    count = lesser.shape[1]
    points, groups = lax.axis_size("ka"), lax.axis_size("ea")
    both = ("ka", "ea")
    bf16, f32 = jnp.bfloat16, jnp.float32
    parity = (lax.axis_index("ka") % 2).astype(jnp.int32).reshape(1)

    def column(block, distance):
        route = [(i, (i + 2 * distance) % points) for i in range(points)]
        return lax.ppermute(block, "ka", route)

    def crossed(block, step, flip):
        route = []
        for k in range(points):
            for e in range(groups):
                if 0 <= e + step < groups:
                    target = k ^ 1 if flip else k
                    route.append((k * groups + e, target * groups + e + step))
        return lax.ppermute(block, both, route)

    pair = (count, orbitals, width)
    one = (1, orbitals, width)
    big = 2 * count * orbitals * width * width

    g_behind = [column(greater[0], distance) for distance in (1, 2)]
    joined = jnp.concatenate([lesser[0], greater[0], coupling[None]], 0)
    flipped, top, factors, g_own = call(
        flip_kernel, "flip", [(pair, bf16), (one, bf16), (pair, bf16), (pair, bf16)], [joined], 2 * big
    )
    g_ahead = [column(g_own, -distance) for distance in (1, 2)]
    above = crossed(flipped, -1, False)
    diagonal = crossed(flipped, -1, True)
    across = crossed(top, 0, True)
    weights = make_weights(jnp.concatenate([offsets, mode_shift]), cotangent, [g_behind[0], top])

    upper = [parity, top, above, across, diagonal, weights]
    ahead, behind = call(upper_far_kernel, "upper_far", [(pair, bf16)] * 2, upper, 6 * big, True)
    ahead, behind = column(ahead, 1), column(behind, -1)

    (acc,) = call(
        lower_near_kernel, "lower_near", [((2, count * orbitals, SMAX * width), f32)],
        [parity, g_behind[0], g_own, g_ahead[0], weights], 12 * big, True,
    )
    own, other, to_above = call(
        lower_far_kernel, "lower_far",
        [((orbitals, width), f32), ((orbitals, width), f32), ((2 * count, orbitals, width), bf16)],
        [parity, g_ahead[1], g_behind[1], weights, acc], 6 * big, True,
    )
    near_ahead, near_behind, here = call(
        upper_near_kernel, "upper_near", [(pair, f32)] * 3, upper, 12 * big, True, [own]
    )
    from_below = crossed(to_above, 1, False)
    (to_across,) = call(merge_kernel, "merge", [(pair, bf16)], [other, from_below], 10**6)
    from_across = crossed(to_across, 0, True)

    behind, ahead = call(pass_kernel, "pass", [(pair, bf16)] * 2, [near_ahead, near_behind, ahead, behind], 10**6)
    behind, ahead = column(behind, -1), column(ahead, 1)
    (grad_lesser,) = call(
        finish_kernel, "finish", [(pair, bf16)],
        [own, from_below, from_across, factors], 2 * big,
    )
    (grad_greater,) = call(total_kernel, "total", [(pair, bf16)], [here, behind, ahead], TAIL)
    return (grad_lesser[None], grad_greater[None])


def solution(mesh):
    in_specs = (P("ka", "ea", None, None), P("ka", "ea", None, None), P(), P(), P(), P())
    out_specs = (P("ka", "ea", None, None), P("ka", "ea", None, None))
    return jax.shard_map(
        per_device, mesh=mesh, in_specs=in_specs, out_specs=out_specs, check_vma=False
    )
```

```python
import functools

import jax
import jax.numpy as jnp
from jax import lax
from jax.experimental import pallas as pl
from jax.experimental.pallas import tpu as pltpu
from jax.sharding import PartitionSpec as P

SMAX = 2
MID = 4
VMEM = 24 * 1024 * 1024
WEIGHTS_VMEM = 44 * 1024 * 1024
TAIL = 10**12


def params():
    return pltpu.CompilerParams(vmem_limit_bytes=VMEM)


def cost(flops, nbytes):
    return pl.CostEstimate(flops=flops // 100, bytes_accessed=nbytes // 100, transcendentals=0)


def resident():
    return pl.BlockSpec(memory_space=pltpu.VMEM)


def scalar():
    return pl.BlockSpec(memory_space=pltpu.SMEM)


def dot(left, right):
    return jnp.dot(left, right, preferred_element_type=jnp.float32)


def dot_t(left, right):
    return lax.dot_general(
        left, right, (((1,), (1,)), ((), ())), preferred_element_type=jnp.float32
    )


def narrow(block):
    return block.astype(jnp.bfloat16)


def weights_kernel(
    facts_ref, p_ref, ahead_ref, behind_ref, w_ref, held_ref, turn_ref, facts, order, arrived, known
):
    slots, modes, orbitals, width = p_ref.shape
    fetch = pltpu.make_async_copy(facts_ref, facts, known)
    fetch.start()
    copies = [pltpu.make_async_copy(p_ref.at[j], held_ref.at[j], arrived.at[j]) for j in range(slots)]
    for copy in copies:
        copy.start()
    row = lax.broadcasted_iota(jnp.int32, (width, width), 0)
    col = lax.broadcasted_iota(jnp.int32, (width, width), 1)
    turn = jnp.where(row == col + orbitals, -1.0, jnp.where(row + orbitals == col, 1.0, 0.0))
    turn_ref[...] = narrow(turn)
    fetch.wait()
    shifts = [facts[slots + m] for m in range(modes)]
    place = jnp.int32(0)
    ends = []
    for shift in range(1, SMAX + 1):
        for m in range(modes):
            found = shifts[m] == shift

            @pl.when(found)
            def _(place=place, m=m):
                order[place] = m

            place = place + found.astype(jnp.int32)
        ends.append(place)
    ordered = [order[m] for m in range(modes)]

    def handle(j, first):
        slot = facts[j]
        blocks = [held_ref[j, mode].astype(jnp.float32) for mode in ordered]
        totals = []
        for run in (blocks[:first], blocks[first:]):
            total = sum(run[1:], run[0]) if run else jnp.zeros((orbitals, width), jnp.float32)
            totals.append(narrow(total))
        turned = narrow(dot(jnp.concatenate(totals, 0), turn_ref[...]))
        for index, total in enumerate(totals):
            w_ref[slot, index, :orbitals, :] = total
            w_ref[slot, index, orbitals:, :] = turned[index * orbitals : (index + 1) * orbitals]

    for first in range(modes + 1):

        @pl.when(ends[0] == first)
        def _(first=first):
            for j, copy in enumerate(copies):
                copy.wait()
                handle(j, first)


def make_weights(facts, cotangent, after):
    slots, modes, orbitals, width = cotangent.shape
    anywhere = pl.BlockSpec(memory_space=pl.ANY)
    main = pl.BlockSpec(memory_space=pltpu.HBM)
    return pl.pallas_call(
        weights_kernel,
        out_shape=jax.ShapeDtypeStruct((slots, SMAX, width, width), jnp.bfloat16),
        in_specs=[main, main, anywhere, anywhere],
        out_specs=resident(),
        scratch_shapes=[
            pltpu.VMEM(cotangent.shape, jnp.bfloat16),
            pltpu.VMEM((width, width), jnp.bfloat16),
            pltpu.SMEM((slots + modes,), jnp.int32),
            pltpu.SMEM((modes,), jnp.int32),
            pltpu.SemaphoreType.DMA((slots,)),
            pltpu.SemaphoreType.DMA,
        ],
        compiler_params=pltpu.CompilerParams(vmem_limit_bytes=WEIGHTS_VMEM),
        cost_estimate=cost(2 * 10**9, 10**7),
        name="weights",
    )(facts, cotangent, *after)


def sandwich(block, factor_ref):
    half_r = narrow(dot_t(factor_ref[0], block))
    half_i = narrow(-dot_t(factor_ref[1], block))
    return narrow(dot(half_r, factor_ref[0]) + dot(half_i, factor_ref[1]))


def flip_kernel(joined_ref, out_ref, top_ref, factor_ref, other_ref):
    count, orbitals, width = out_ref.shape
    other_ref[...] = joined_ref[count : 2 * count]
    turned = joined_ref[2 * count].astype(jnp.float32).T
    c_r, c_i = narrow(turned[:orbitals]), narrow(turned[orbitals:])
    row = lax.broadcasted_iota(jnp.int32, (orbitals, width), 0)
    col = lax.broadcasted_iota(jnp.int32, (orbitals, width), 1)
    left = narrow(jnp.where(row == col, 1.0, 0.0))
    right = narrow(jnp.where(row + orbitals == col, 1.0, 0.0))
    factor_ref[0] = narrow(dot(c_r, left) - dot(c_i, right))
    factor_ref[1] = narrow(-dot(c_i, left) - dot(c_r, right))
    for index in range(count):
        result = sandwich(joined_ref[index], factor_ref)
        out_ref[index] = result
        if index == count - 1:
            top_ref[0] = result


def finish_kernel(own_ref, below_ref, across_ref, factor_ref, out_ref):
    wide = lambda ref, index: ref[index].astype(jnp.float32)
    first = wide(below_ref, 0) + wide(across_ref, 0)
    second = own_ref[...] + wide(below_ref, 1) + wide(across_ref, 1)
    out_ref[0] = sandwich(narrow(first), factor_ref)
    out_ref[1] = sandwich(narrow(second), factor_ref)


def slot_weights(w_ref, slot):
    block = w_ref[slot]
    return block.reshape(block.shape[0] * block.shape[1], block.shape[2])


def flat(ref):
    block = ref[...]
    return block.reshape(block.shape[0] * block.shape[1], block.shape[2])


def beside(blocks):
    return jnp.concatenate(blocks, 1)


def lower_near_kernel(parity_ref, behind_ref, own_ref, ahead_ref, w_ref, acc_ref):
    even = parity_ref[0] == 0
    blocks = beside([flat(behind_ref), flat(own_ref), flat(ahead_ref)])
    for which in range(2):
        slots = [MID - 2 * column for column in (-1, 0, 1)]
        if which == 1:
            slots = [jnp.where(even, slot + 1, slot - 1) for slot in slots]
        acc_ref[which] = dot_t(blocks, beside([slot_weights(w_ref, slot) for slot in slots]))


def lower_far_kernel(parity_ref, behind_ref, ahead_ref, w_ref, acc_ref, own_ref, other_ref, above_ref):
    even = parity_ref[0] == 0
    behind, ahead = flat(behind_ref), flat(ahead_ref)
    chosen = jnp.where(even, ahead, behind)
    slot = jnp.where(even, 1, 2 * MID - 1)
    rows, width = own_ref.shape
    both = beside([slot_weights(w_ref, 0), slot_weights(w_ref, 2 * MID)])
    same = acc_ref[0] + dot_t(beside([ahead, behind]), both)
    other = acc_ref[1] + dot_t(chosen, slot_weights(w_ref, slot))
    own_ref[...] = same[:rows, :width]
    other_ref[...] = other[:rows, :width]
    for index, sums in enumerate((same, other)):
        above_ref[2 * index] = narrow(sums[rows:, :width] + sums[:rows, width:])
        above_ref[2 * index + 1] = narrow(sums[rows:, width:])


def merge_kernel(other_ref, below_ref, across_ref):
    across_ref[0] = below_ref[2]
    across_ref[1] = narrow(other_ref[...] + below_ref[3].astype(jnp.float32))


def stack_pairs(first_ref, pair_ref):
    first = first_ref[first_ref.shape[0] - 1]
    return [jnp.concatenate([first, pair_ref[0]], 0), flat(pair_ref)]


def store(ref, rows, kind=None):
    height = ref.shape[1]
    for index in range(ref.shape[0]):
        part = rows[index * height : (index + 1) * height]
        ref[index] = part if kind is None else part.astype(kind)


def upper_far_kernel(parity_ref, own_ref, above_ref, across_ref, diagonal_ref, w_ref, behind_ref, ahead_ref):
    even = parity_ref[0] == 0
    width = w_ref.shape[-1]
    same = beside(stack_pairs(own_ref, above_ref))
    other = beside(stack_pairs(across_ref, diagonal_ref))
    extra = dot(other, slot_weights(w_ref, jnp.where(even, 1, 2 * MID - 1)))
    sums = dot(same, beside([slot_weights(w_ref, 0), slot_weights(w_ref, 2 * MID)]))
    store(ahead_ref, sums[:, :width] + jnp.where(even, extra, 0.0), jnp.bfloat16)
    store(behind_ref, sums[:, width:] + jnp.where(even, 0.0, extra), jnp.bfloat16)


def upper_near_kernel(
    parity_ref, own_ref, above_ref, across_ref, diagonal_ref, w_ref, after_ref, ahead_ref, behind_ref, here_ref
):
    even = parity_ref[0] == 0
    width = w_ref.shape[-1]
    blocks = beside(stack_pairs(own_ref, above_ref) + stack_pairs(across_ref, diagonal_ref))
    same = [MID - 2 * column for column in (1, -1, 0)]
    other = [jnp.where(even, slot + 1, slot - 1) for slot in same]
    weights = jnp.concatenate(
        [beside([slot_weights(w_ref, slot) for slot in slots]) for slots in (same, other)], 0
    )
    sums = dot(blocks, weights)
    for index, ref in enumerate((ahead_ref, behind_ref, here_ref)):
        store(ref, sums[:, index * width : (index + 1) * width])


def pass_kernel(near_ahead, near_behind, behind_ref, ahead_ref, ahead_out, behind_out):
    ahead_out[...] = narrow(near_ahead[...] + ahead_ref[...].astype(jnp.float32))
    behind_out[...] = narrow(near_behind[...] + behind_ref[...].astype(jnp.float32))


def total_kernel(here_ref, ahead_ref, behind_ref, out_ref):
    arrived = ahead_ref[...].astype(jnp.float32) + behind_ref[...].astype(jnp.float32)
    out_ref[...] = narrow(here_ref[...] + arrived)


def call(kernel, name, outs, args, flops, has_scalar=False, after=()):
    specs = [resident() for _ in args] + [pl.BlockSpec(memory_space=pl.ANY) for _ in after]
    if has_scalar:
        specs[0] = scalar()
    nbytes = 4 * 10**6
    return pl.pallas_call(
        kernel,
        out_shape=[jax.ShapeDtypeStruct(s, d) for s, d in outs],
        in_specs=specs,
        out_specs=[resident() for _ in outs],
        compiler_params=params(),
        cost_estimate=cost(flops, nbytes),
        name=name,
    )(*args, *after)


def per_device(lesser, greater, coupling, cotangent, offsets, mode_shift):
    orbitals, width = coupling.shape
    count = lesser.shape[1]
    points, groups = lax.axis_size("ka"), lax.axis_size("ea")
    both = ("ka", "ea")
    bf16, f32 = jnp.bfloat16, jnp.float32
    parity = (lax.axis_index("ka") % 2).astype(jnp.int32).reshape(1)

    def column(block, distance):
        route = [(i, (i + 2 * distance) % points) for i in range(points)]
        return lax.ppermute(block, "ka", route)

    def crossed(block, step, flip):
        route = []
        for k in range(points):
            for e in range(groups):
                if 0 <= e + step < groups:
                    target = k ^ 1 if flip else k
                    route.append((k * groups + e, target * groups + e + step))
        return lax.ppermute(block, both, route)

    pair = (count, orbitals, width)
    one = (1, orbitals, width)
    big = 2 * count * orbitals * width * width

    g_behind = [column(greater[0], 1)]
    g_behind.append(column(g_behind[0], 1))
    joined = jnp.concatenate([lesser[0], greater[0], coupling[None]], 0)
    flipped, top, factors, g_own = call(
        flip_kernel, "flip", [(pair, bf16), (one, bf16), (pair, bf16), (pair, bf16)], [joined], 2 * big
    )
    g_ahead = [column(g_own, -1)]
    g_ahead.append(column(g_ahead[0], -1))
    above = crossed(flipped, -1, False)
    diagonal = crossed(flipped, -1, True)
    across = crossed(top, 0, True)
    weights = make_weights(jnp.concatenate([offsets, mode_shift]), cotangent, [g_behind[0], top])

    upper = [parity, top, above, across, diagonal, weights]
    behind, ahead = call(upper_far_kernel, "upper_far", [(pair, bf16)] * 2, upper, 6 * big, True)
    ahead, behind = column(ahead, 1), column(behind, -1)

    (acc,) = call(
        lower_near_kernel, "lower_near", [((2, count * orbitals, SMAX * width), f32)],
        [parity, g_behind[0], g_own, g_ahead[0], weights], 12 * big, True,
    )
    own, other, to_above = call(
        lower_far_kernel, "lower_far",
        [((orbitals, width), f32), ((orbitals, width), f32), ((2 * count, orbitals, width), bf16)],
        [parity, g_behind[1], g_ahead[1], weights, acc], 6 * big, True,
    )
    near_ahead, near_behind, here = call(
        upper_near_kernel, "upper_near", [(pair, f32)] * 3, upper, 12 * big, True, [own]
    )
    from_below = crossed(to_above, 1, False)
    (to_across,) = call(merge_kernel, "merge", [(pair, bf16)], [other, from_below], 10**6)
    from_across = crossed(to_across, 0, True)

    ahead, behind = call(pass_kernel, "pass", [(pair, bf16)] * 2, [near_ahead, near_behind, behind, ahead], 10**6)
    behind, ahead = column(behind, -1), column(ahead, 1)
    (grad_lesser,) = call(
        finish_kernel, "finish", [(pair, bf16)],
        [own, from_below, from_across, factors], 2 * big,
    )
    (grad_greater,) = call(total_kernel, "total", [(pair, bf16)], [here, ahead, behind], TAIL)
    return (grad_lesser[None], grad_greater[None])


def solution(mesh):
    in_specs = (P("ka", "ea", None, None), P("ka", "ea", None, None), P(), P(), P(), P())
    out_specs = (P("ka", "ea", None, None), P("ka", "ea", None, None))
    return jax.shard_map(
        per_device, mesh=mesh, in_specs=in_specs, out_specs=out_specs, check_vma=False
    )
```

```python
import functools

import jax
import jax.numpy as jnp
from jax import lax
from jax.experimental import pallas as pl
from jax.experimental.pallas import tpu as pltpu
from jax.sharding import PartitionSpec as P

SMAX = 2
MID = 4
FAR = (0, 1, 7, 8)
NEAR = (1, 2, 3, 4, 5, 6, 7)
VMEM = 24 * 1024 * 1024
WEIGHTS_VMEM = {4: 48, 7: 44}
TAIL = 10**12


def params():
    return pltpu.CompilerParams(vmem_limit_bytes=VMEM)


def cost(flops, nbytes):
    return pl.CostEstimate(flops=flops // 100, bytes_accessed=nbytes // 100, transcendentals=0)


def resident():
    return pl.BlockSpec(memory_space=pltpu.VMEM)


def scalar():
    return pl.BlockSpec(memory_space=pltpu.SMEM)


def dot(left, right):
    return jnp.dot(left, right, preferred_element_type=jnp.float32)


def dot_t(left, right):
    return lax.dot_general(
        left, right, (((1,), (1,)), ((), ())), preferred_element_type=jnp.float32
    )


def narrow(block):
    return block.astype(jnp.bfloat16)


def weights_kernel(
    wanted, facts_ref, p_ref, first_ref, second_ref, w_ref, held_ref, turn_ref, facts, order, place_of, arrived, known
):
    slots, modes, orbitals, width = p_ref.shape
    fetch = pltpu.make_async_copy(facts_ref, facts, known)
    fetch.start()
    fetch.wait()
    for j in range(slots):
        place_of[facts[j]] = jnp.int32(j)
    copies = [
        pltpu.make_async_copy(p_ref.at[place_of[slot]], held_ref.at[i], arrived.at[i])
        for i, slot in enumerate(wanted)
    ]
    for copy in copies:
        copy.start()
    row = lax.broadcasted_iota(jnp.int32, (width, width), 0)
    col = lax.broadcasted_iota(jnp.int32, (width, width), 1)
    turn = jnp.where(row == col + orbitals, -1.0, jnp.where(row + orbitals == col, 1.0, 0.0))
    turn_ref[...] = narrow(turn)
    shifts = [facts[slots + m] for m in range(modes)]
    place = jnp.int32(0)
    ends = []
    for shift in range(1, SMAX + 1):
        for m in range(modes):
            found = shifts[m] == shift

            @pl.when(found)
            def _(place=place, m=m):
                order[place] = m

            place = place + found.astype(jnp.int32)
        ends.append(place)
    ordered = [order[m] for m in range(modes)]

    def handle(j, first):
        blocks = [held_ref[j, mode].astype(jnp.float32) for mode in ordered]
        totals = []
        for run in (blocks[:first], blocks[first:]):
            total = sum(run[1:], run[0]) if run else jnp.zeros((orbitals, width), jnp.float32)
            totals.append(narrow(total))
        turned = narrow(dot(jnp.concatenate(totals, 0), turn_ref[...]))
        for index, total in enumerate(totals):
            w_ref[j, index, :orbitals, :] = total
            w_ref[j, index, orbitals:, :] = turned[index * orbitals : (index + 1) * orbitals]

    for first in range(modes + 1):

        @pl.when(ends[0] == first)
        def _(first=first):
            for j, copy in enumerate(copies):
                copy.wait()
                handle(j, first)


def make_weights(facts, cotangent, wanted, after):
    slots, modes, orbitals, width = cotangent.shape
    count = len(wanted)
    anywhere = pl.BlockSpec(memory_space=pl.ANY)
    main = pl.BlockSpec(memory_space=pltpu.HBM)
    return pl.pallas_call(
        functools.partial(weights_kernel, wanted),
        out_shape=jax.ShapeDtypeStruct((count, SMAX, width, width), jnp.bfloat16),
        in_specs=[main, main, anywhere, anywhere],
        out_specs=resident(),
        scratch_shapes=[
            pltpu.VMEM((count,) + cotangent.shape[1:], jnp.bfloat16),
            pltpu.VMEM((width, width), jnp.bfloat16),
            pltpu.SMEM((slots + modes,), jnp.int32),
            pltpu.SMEM((modes,), jnp.int32),
            pltpu.SMEM((slots,), jnp.int32),
            pltpu.SemaphoreType.DMA((count,)),
            pltpu.SemaphoreType.DMA,
        ],
        compiler_params=pltpu.CompilerParams(vmem_limit_bytes=WEIGHTS_VMEM[count] * 1024 * 1024),
        cost_estimate=cost(2 * 10**9, 10**7),
        name="weights",
    )(facts, cotangent, *after)


def sandwich(block, factor_ref):
    half_r = narrow(dot_t(factor_ref[0], block))
    half_i = narrow(-dot_t(factor_ref[1], block))
    return narrow(dot(half_r, factor_ref[0]) + dot(half_i, factor_ref[1]))


def flip_kernel(joined_ref, out_ref, top_ref, factor_ref, other_ref):
    count, orbitals, width = out_ref.shape
    other_ref[...] = joined_ref[count : 2 * count]
    turned = joined_ref[2 * count].astype(jnp.float32).T
    c_r, c_i = narrow(turned[:orbitals]), narrow(turned[orbitals:])
    row = lax.broadcasted_iota(jnp.int32, (orbitals, width), 0)
    col = lax.broadcasted_iota(jnp.int32, (orbitals, width), 1)
    left = narrow(jnp.where(row == col, 1.0, 0.0))
    right = narrow(jnp.where(row + orbitals == col, 1.0, 0.0))
    factor_ref[0] = narrow(dot(c_r, left) - dot(c_i, right))
    factor_ref[1] = narrow(-dot(c_i, left) - dot(c_r, right))
    for index in range(count):
        result = sandwich(joined_ref[index], factor_ref)
        out_ref[index] = result
        if index == count - 1:
            top_ref[0] = result


def finish_kernel(own_ref, below_ref, across_ref, factor_ref, out_ref):
    wide = lambda ref, index: ref[index].astype(jnp.float32)
    first = wide(below_ref, 0) + wide(across_ref, 0)
    second = own_ref[...] + wide(below_ref, 1) + wide(across_ref, 1)
    out_ref[0] = sandwich(narrow(first), factor_ref)
    out_ref[1] = sandwich(narrow(second), factor_ref)


def slot_weights(w_ref, slot):
    block = w_ref[slot]
    return block.reshape(block.shape[0] * block.shape[1], block.shape[2])


def flat(ref):
    block = ref[...]
    return block.reshape(block.shape[0] * block.shape[1], block.shape[2])


def beside(blocks):
    return jnp.concatenate(blocks, 1)


def lower_near_kernel(parity_ref, behind_ref, own_ref, ahead_ref, w_ref, acc_ref):
    even = parity_ref[0] == 0
    blocks = beside([flat(behind_ref), flat(own_ref), flat(ahead_ref)])
    for which in range(2):
        slots = [MID - NEAR[0] - 2 * column for column in (-1, 0, 1)]
        if which == 1:
            slots = [jnp.where(even, slot + 1, slot - 1) for slot in slots]
        acc_ref[which] = dot_t(blocks, beside([slot_weights(w_ref, slot) for slot in slots]))


def lower_far_kernel(parity_ref, behind_ref, ahead_ref, w_ref, acc_ref, own_ref, other_ref, above_ref):
    even = parity_ref[0] == 0
    behind, ahead = flat(behind_ref), flat(ahead_ref)
    chosen = jnp.where(even, ahead, behind)
    slot = jnp.where(even, 1, 2)
    rows, width = own_ref.shape
    both = beside([slot_weights(w_ref, 0), slot_weights(w_ref, 3)])
    same = acc_ref[0] + dot_t(beside([ahead, behind]), both)
    other = acc_ref[1] + dot_t(chosen, slot_weights(w_ref, slot))
    own_ref[...] = same[:rows, :width]
    other_ref[...] = other[:rows, :width]
    for index, sums in enumerate((same, other)):
        above_ref[2 * index] = narrow(sums[rows:, :width] + sums[:rows, width:])
        above_ref[2 * index + 1] = narrow(sums[rows:, width:])


def merge_kernel(other_ref, below_ref, across_ref):
    across_ref[0] = below_ref[2]
    across_ref[1] = narrow(other_ref[...] + below_ref[3].astype(jnp.float32))


def stack_pairs(first_ref, pair_ref):
    first = first_ref[first_ref.shape[0] - 1]
    return [jnp.concatenate([first, pair_ref[0]], 0), flat(pair_ref)]


def store(ref, rows, kind=None):
    height = ref.shape[1]
    for index in range(ref.shape[0]):
        part = rows[index * height : (index + 1) * height]
        ref[index] = part if kind is None else part.astype(kind)


def upper_far_kernel(parity_ref, own_ref, above_ref, across_ref, diagonal_ref, w_ref, behind_ref, ahead_ref):
    even = parity_ref[0] == 0
    width = w_ref.shape[-1]
    same = beside(stack_pairs(own_ref, above_ref))
    other = beside(stack_pairs(across_ref, diagonal_ref))
    extra = dot(other, slot_weights(w_ref, jnp.where(even, 1, 2)))
    sums = dot(same, beside([slot_weights(w_ref, 0), slot_weights(w_ref, 3)]))
    store(ahead_ref, sums[:, :width] + jnp.where(even, extra, 0.0), jnp.bfloat16)
    store(behind_ref, sums[:, width:] + jnp.where(even, 0.0, extra), jnp.bfloat16)


def upper_near_kernel(
    parity_ref, own_ref, above_ref, across_ref, diagonal_ref, w_ref, after_ref, ahead_ref, behind_ref, here_ref
):
    even = parity_ref[0] == 0
    width = w_ref.shape[-1]
    blocks = beside(stack_pairs(own_ref, above_ref) + stack_pairs(across_ref, diagonal_ref))
    same = [MID - NEAR[0] - 2 * column for column in (1, -1, 0)]
    other = [jnp.where(even, slot + 1, slot - 1) for slot in same]
    weights = jnp.concatenate(
        [beside([slot_weights(w_ref, slot) for slot in slots]) for slots in (same, other)], 0
    )
    sums = dot(blocks, weights)
    for index, ref in enumerate((ahead_ref, behind_ref, here_ref)):
        store(ref, sums[:, index * width : (index + 1) * width])


def pass_kernel(near_ahead, near_behind, behind_ref, ahead_ref, ahead_out, behind_out):
    ahead_out[...] = narrow(near_ahead[...] + ahead_ref[...].astype(jnp.float32))
    behind_out[...] = narrow(near_behind[...] + behind_ref[...].astype(jnp.float32))


def total_kernel(here_ref, ahead_ref, behind_ref, out_ref):
    arrived = ahead_ref[...].astype(jnp.float32) + behind_ref[...].astype(jnp.float32)
    out_ref[...] = narrow(here_ref[...] + arrived)


def call(kernel, name, outs, args, flops, has_scalar=False, after=()):
    specs = [resident() for _ in args] + [pl.BlockSpec(memory_space=pl.ANY) for _ in after]
    if has_scalar:
        specs[0] = scalar()
    nbytes = 4 * 10**6
    return pl.pallas_call(
        kernel,
        out_shape=[jax.ShapeDtypeStruct(s, d) for s, d in outs],
        in_specs=specs,
        out_specs=[resident() for _ in outs],
        compiler_params=params(),
        cost_estimate=cost(flops, nbytes),
        name=name,
    )(*args, *after)


def per_device(lesser, greater, coupling, cotangent, offsets, mode_shift):
    orbitals, width = coupling.shape
    count = lesser.shape[1]
    points, groups = lax.axis_size("ka"), lax.axis_size("ea")
    both = ("ka", "ea")
    bf16, f32 = jnp.bfloat16, jnp.float32
    parity = (lax.axis_index("ka") % 2).astype(jnp.int32).reshape(1)

    def column(block, distance):
        route = [(i, (i + 2 * distance) % points) for i in range(points)]
        return lax.ppermute(block, "ka", route)

    def crossed(block, step, flip):
        route = []
        for k in range(points):
            for e in range(groups):
                if 0 <= e + step < groups:
                    target = k ^ 1 if flip else k
                    route.append((k * groups + e, target * groups + e + step))
        return lax.ppermute(block, both, route)

    pair = (count, orbitals, width)
    one = (1, orbitals, width)
    big = 2 * count * orbitals * width * width

    g_behind = [column(greater[0], 1)]
    g_behind.append(column(g_behind[0], 1))
    joined = jnp.concatenate([lesser[0], greater[0], coupling[None]], 0)
    flipped, top, factors, g_own = call(
        flip_kernel, "flip", [(pair, bf16), (one, bf16), (pair, bf16), (pair, bf16)], [joined], 2 * big
    )
    g_ahead = [column(g_own, -1)]
    g_ahead.append(column(g_ahead[0], -1))
    above = crossed(flipped, -1, False)
    diagonal = crossed(flipped, -1, True)
    across = crossed(top, 0, True)
    facts = jnp.concatenate([offsets, mode_shift])
    weights_far = make_weights(facts, cotangent, FAR, [g_behind[0], top])

    upper = [parity, top, above, across, diagonal]
    behind, ahead = call(upper_far_kernel, "upper_far", [(pair, bf16)] * 2, upper + [weights_far], 6 * big, True)
    sent = [behind, ahead]
    ahead, behind = column(ahead, 1), column(behind, -1)

    weights_near = make_weights(facts, cotangent, NEAR, sent)
    (acc,) = call(
        lower_near_kernel, "lower_near", [((2, count * orbitals, SMAX * width), f32)],
        [parity, g_behind[0], g_own, g_ahead[0], weights_near], 12 * big, True,
    )
    own, other, to_above = call(
        lower_far_kernel, "lower_far",
        [((orbitals, width), f32), ((orbitals, width), f32), ((2 * count, orbitals, width), bf16)],
        [parity, g_behind[1], g_ahead[1], weights_far, acc], 6 * big, True,
    )
    near_ahead, near_behind, here = call(
        upper_near_kernel, "upper_near", [(pair, f32)] * 3, upper + [weights_near], 12 * big, True, [own]
    )
    from_below = crossed(to_above, 1, False)
    (to_across,) = call(merge_kernel, "merge", [(pair, bf16)], [other, from_below], 10**6)
    from_across = crossed(to_across, 0, True)

    ahead, behind = call(pass_kernel, "pass", [(pair, bf16)] * 2, [near_ahead, near_behind, behind, ahead], 10**6)
    behind, ahead = column(behind, -1), column(ahead, 1)
    (grad_lesser,) = call(
        finish_kernel, "finish", [(pair, bf16)],
        [own, from_below, from_across, factors], 2 * big,
    )
    (grad_greater,) = call(total_kernel, "total", [(pair, bf16)], [here, ahead, behind], TAIL)
    return (grad_lesser[None], grad_greater[None])


def solution(mesh):
    in_specs = (P("ka", "ea", None, None), P("ka", "ea", None, None), P(), P(), P(), P())
    out_specs = (P("ka", "ea", None, None), P("ka", "ea", None, None))
    return jax.shard_map(
        per_device, mesh=mesh, in_specs=in_specs, out_specs=out_specs, check_vma=False
    )
```
